32 devices in a mesh: parts: 2 (over y), seq: 4 (over z), head: 2 (over x), sub: 2 (over core).
Axes of the slice: x: 2, y: 2, z: 4, core: 2. Of those that a mesh axis runs over, the one named last changes fastest.
Arguments:
- queries: bfloat16 [8192, 8192], P(('parts', 'seq'), ('head', 'sub')), parts along dimension 0, may hold values from -7 to 7
- keys: bfloat16 [8192, 1024], P(('parts', 'seq'), 'head'), parts along dimension 0, may hold values from -4 to 4
- values: bfloat16 [8192, 1024], P(('parts', 'seq'), 'head'), parts along dimension 0, may hold values from -5 to 5
- out_grad: bfloat16 [8192, 8192], P(('parts', 'seq'), ('head', 'sub')), parts along dimension 0, may hold values from -12 to 12
- prompt_group: int32 [8], P('parts'), parts along dimension 0, may hold values from 0 to 3, each once
- slot_group: int32 [8, 2], P('parts'), parts along dimension 0, may hold values from 0 to 3, as said below
- resp_len: int32 [8, 2], P(('parts', 'seq')), parts along dimension 0, may hold values from 128 to 256, as said below
Outputs:
- query_grad: bfloat16 [8192, 8192], P(('parts', 'seq'), ('head', 'sub')), parts along dimension 0
- key_grad: bfloat16 [8192, 1024], P(('parts', 'seq'), 'head'), parts along dimension 0
- value_grad: bfloat16 [8192, 1024], P(('parts', 'seq'), 'head'), parts along dimension 0
The draws below stay inside these ranges and needn't reach their ends.
There are 2 independent parts, one for each index of `parts`. The reference program is written for one: setup_inputs(seed, part) draws one part's arguments, and reference() takes and returns one part's arrays. A program takes and returns all parts, laid end to end along the dimension named above; each array names one. Nothing has to cross between parts.
Inputs may be any that keep to these rules, and one draw needn't show every extreme that they name: `slot_group`: each group id appears in exactly two of the 8 slots. `resp_len`: some slot has exactly 256. `prompt_group`: each group's prompt is in exactly one block.
All inputs are finite; a program needn't handle non-finite values.
Results may differ from the reference program's by a relative error of at most 0.0088.
Values may be sent and summed in bfloat16 or wider, within the bound.
A program may use at most 128 MiB of HBM per device.

```python
import math
import jax
import jax.numpy as jnp
from jax import lax

HQ = 64
KVH = 8
HD = 128
PROMPT = 512
RESP = 256
TOKENS = 4096
N_SEQ = 4


def draw_queries(key, part):
    key = jax.random.fold_in(key, 1)
    base_key = jax.random.fold_in(key, 0)
    total_rows = N_SEQ * (PROMPT + 2 * RESP)
    drawn = jnp.clip(1.5 * jax.random.normal(base_key, (total_rows, HQ * HD), jnp.float32), -6.0, 6.0)
    return drawn.astype(jnp.bfloat16)


def draw_keys(key, part):
    key = jax.random.fold_in(key, 2)
    total_rows = N_SEQ * (PROMPT + 2 * RESP)
    drawn = jnp.clip(jax.random.normal(key, (total_rows, KVH * HD), jnp.float32), -4.0, 4.0)
    return drawn.astype(jnp.bfloat16)


def draw_slot_group(key, part):
    key = jax.random.fold_in(key, 3)
    order = jax.random.permutation(key, 2 * N_SEQ)
    return (order // 2).reshape(N_SEQ, 2).astype(jnp.int32)


def draw_resp_len(key, part):
    key = jax.random.fold_in(key, 4)
    length_key, longest_key = jax.random.split(key)
    lengths = jax.random.randint(length_key, (2 * N_SEQ,), RESP // 2, RESP + 1, jnp.int32)
    longest = jax.random.randint(longest_key, (), 0, 2 * N_SEQ, jnp.int32)
    lengths = jnp.where(jnp.arange(2 * N_SEQ, dtype=jnp.int32) == longest, RESP, lengths)
    return lengths.reshape(N_SEQ, 2).astype(jnp.int32)


def shard_levels(rng, shape, cuts, low, largest):
    def one(dim, shards_of):
        steps = jax.random.uniform(jax.random.fold_in(jax.random.fold_in(rng, 6), dim), (shards_of,), jnp.float32, low / len(cuts), largest / len(cuts))
        return jnp.repeat(jnp.exp(steps), shape[dim] // shards_of).reshape((-1,) + (1,) * (len(shape) - dim - 1))

    loudness = one(*cuts[0])
    for cut in cuts[1:]:
        loudness = loudness * one(*cut)
    return loudness


def gaussian(stream_key, shape, scale, limit, cuts=(), kind=jnp.bfloat16):
    loudness = shard_levels(stream_key, shape, cuts, -0.22, 0.18) if cuts else 1.0
    values = jax.random.normal(stream_key, shape, jnp.float32) * scale * loudness
    return jnp.minimum(jnp.maximum(values, -limit), limit).astype(kind)


def setup_inputs(seed: int = 0, part: int = 0) -> dict:
    key_of = jax.random.split(jax.random.key(seed), 8)
    part_splits = jax.random.split(jax.random.fold_in(key_of[7], part), 8)
    return {
        "queries": draw_queries(jax.random.fold_in(jax.random.fold_in(key_of[7], part), 71), part),
        "keys": draw_keys(jax.random.fold_in(jax.random.fold_in(key_of[7], part), 71), part),
        "values": gaussian(part_splits[2], (TOKENS, KVH * HD), 1.0, 5.0, ((0, 4), (1, 2))),
        "out_grad": gaussian(part_splits[3], (TOKENS, HQ * HD), 2.0, 12.0, ((0, 4), (1, 4))),
        "prompt_group": jax.random.permutation(part_splits[4], N_SEQ).astype(jnp.int32),
        "slot_group": draw_slot_group(jax.random.fold_in(jax.random.fold_in(key_of[7], part), 71), part),
        "resp_len": draw_resp_len(jax.random.fold_in(jax.random.fold_in(key_of[7], part), 71), part),
    }


def rounded(array):
    return lax.optimization_barrier(array.astype(jnp.bfloat16)).astype(jnp.float32)

def segment_grads(query, grad_out, key_rows, value_rows, allowed):
    amount = query.shape[0]
    extent = key_rows.shape[0]
    kv_heads = key_rows.shape[1] // HD
    shared = query.shape[1] // (kv_heads * HD)
    scale = 1.0 / math.sqrt(HD)
    query_heads = query.astype(jnp.float32).reshape(amount, kv_heads, shared, HD)
    grad_heads = grad_out.astype(jnp.float32).reshape(amount, kv_heads, shared, HD)
    key_heads = key_rows.astype(jnp.float32).reshape(extent, kv_heads, HD)
    value_heads = value_rows.astype(jnp.float32).reshape(extent, kv_heads, HD)
    scores = jnp.einsum('qkgd,jkd->kgqj', query_heads, key_heads) * scale
    scores = jnp.where(allowed, scores, -jnp.inf)
    highest = lax.optimization_barrier(jnp.max(scores, axis=-1, keepdims=True))
    weights = jnp.exp(scores - highest)
    chances = rounded(weights / lax.optimization_barrier(jnp.sum(weights, axis=-1, keepdims=True)))
    attended = jnp.einsum('kgqj,jkd->kgqd', chances, value_heads)
    grad_chance = jnp.einsum('qkgd,jkd->kgqj', grad_heads, value_heads)
    row_dot = lax.optimization_barrier(jnp.sum(jnp.transpose(grad_heads, (1, 2, 0, 3)) * attended, axis=-1, keepdims=True))
    grad_score = rounded(chances * (grad_chance - row_dot) * scale)
    grad_query = jnp.einsum('kgqj,jkd->qkgd', grad_score, key_heads).reshape(amount, -1)
    grad_key = jnp.einsum('kgqj,qkgd->jkd', grad_score, query_heads).reshape(extent, -1)
    grad_value = jnp.einsum('kgqj,qkgd->jkd', chances, grad_heads).reshape(extent, -1)
    return (grad_query, grad_key, grad_value)

def reference(queries, keys, values, out_grad, prompt_group, slot_group, resp_len):
    span = PROMPT + 2 * RESP
    peers = jnp.arange(N_SEQ, dtype=jnp.int32)
    owners = lax.optimization_barrier(jnp.sum(peers[:, None] * (prompt_group[:, None] == peers[None, :]).astype(jnp.int32), axis=0))
    flat_group = slot_group.reshape(-1)
    flat_length = resp_len.reshape(-1)
    prompt_index = jnp.arange(PROMPT)
    prompt_mask = prompt_index[None, :] <= prompt_index[:, None]
    reply_index = jnp.arange(RESP)
    key_index = jnp.arange(PROMPT + RESP)
    reply_mask = (key_index[None, :] < PROMPT) | (key_index[None, :] - PROMPT <= reply_index[:, None])

    def take_rows(array, start):
        return lax.dynamic_slice_in_dim(array, start, PROMPT, 0)

    def take_reply(array, start):
        return lax.dynamic_slice_in_dim(array, start, RESP, 0)

    def visit(group_id, carry):
        query_all, key_all, value_all = carry
        hits = (flat_group == group_id).astype(jnp.int32)
        first = jnp.argmax(hits).astype(jnp.int32)
        second = (2 * N_SEQ - 1 - jnp.argmax(hits[::-1])).astype(jnp.int32)
        prompt_start = (owners[group_id] * span).astype(jnp.int32)
        prompt_keys = take_rows(keys, prompt_start)
        prompt_values = take_rows(values, prompt_start)
        grad_query, key_sum, value_sum = segment_grads(take_rows(queries, prompt_start), take_rows(out_grad, prompt_start), prompt_keys, prompt_values, prompt_mask)
        query_all = lax.dynamic_update_slice_in_dim(query_all, grad_query.astype(jnp.bfloat16), prompt_start, 0)
        for slot_index in (first, second):
            device_block = slot_index // 2
            position = slot_index % 2
            start = (device_block * span + PROMPT + position * RESP).astype(jnp.int32)
            live = (reply_index < flat_length[slot_index])[:, None]
            grad_live = jnp.where(live, take_reply(out_grad, start), jnp.zeros((), jnp.bfloat16))
            joined_keys = jnp.concatenate([prompt_keys, take_reply(keys, start)], axis=0)
            joined_values = jnp.concatenate([prompt_values, take_reply(values, start)], axis=0)
            reply_query, reply_key, reply_value = segment_grads(take_reply(queries, start), grad_live, joined_keys, joined_values, reply_mask)
            key_sum = key_sum + reply_key[:PROMPT]
            value_sum = value_sum + reply_value[:PROMPT]
            query_all = lax.dynamic_update_slice_in_dim(query_all, reply_query.astype(jnp.bfloat16), start, 0)
            key_all = lax.dynamic_update_slice_in_dim(key_all, reply_key[PROMPT:].astype(jnp.bfloat16), start, 0)
            value_all = lax.dynamic_update_slice_in_dim(value_all, reply_value[PROMPT:].astype(jnp.bfloat16), start, 0)
        key_all = lax.dynamic_update_slice_in_dim(key_all, key_sum.astype(jnp.bfloat16), prompt_start, 0)
        value_all = lax.dynamic_update_slice_in_dim(value_all, value_sum.astype(jnp.bfloat16), prompt_start, 0)
        return (query_all, key_all, value_all)
    start_state = (jnp.zeros(queries.shape, jnp.bfloat16), jnp.zeros(keys.shape, jnp.bfloat16), jnp.zeros(values.shape, jnp.bfloat16))
    finished = lax.fori_loop(0, N_SEQ, visit, start_state)
    return (finished[0], finished[1], finished[2])
```

```python
import functools
import math

import jax
import jax.numpy as jnp
from jax import lax
from jax.experimental import pallas as pl
from jax.experimental.pallas import tpu as pltpu
from jax.sharding import PartitionSpec as P

HQ = 64
KVH = 8
HD = 128
PROMPT = 512
RESP = 256
SCALE = 1.0 / math.sqrt(HD)
EXP2_SCALE = SCALE * math.log2(math.e)
ROW_ROW = (((1,), (1,)), ((), ()))
COL_COL = (((0,), (0,)), ((), ()))


def attend(query, grad, key, value):
    extent, amount = key.shape[0], query.shape[0]
    scores = lax.dot_general(key, query, ROW_ROW, preferred_element_type=jnp.float32)
    grad_chance = lax.dot_general(value, grad, ROW_ROW, preferred_element_type=jnp.float32)
    key_index = lax.broadcasted_iota(jnp.int32, (amount, amount), 0)
    query_index = lax.broadcasted_iota(jnp.int32, (amount, amount), 1)
    last = jnp.where(key_index <= query_index, scores[extent - amount :], -jnp.inf)
    if extent > amount:
        scores = jnp.concatenate([scores[: extent - amount], last], axis=0)
    else:
        scores = last
    highest = jnp.max(scores, axis=0, keepdims=True)
    weights = jnp.exp2((scores - highest) * EXP2_SCALE)
    inverse = 1.0 / jnp.sum(weights, axis=0, keepdims=True)
    row_dot = jnp.sum(weights * grad_chance, axis=0, keepdims=True) * inverse
    chances = (weights * inverse).astype(jnp.bfloat16)
    grad_score = chances * (grad_chance - row_dot).astype(jnp.bfloat16)
    key_term = jnp.dot(grad_score, query, preferred_element_type=jnp.float32) * SCALE
    value_term = jnp.dot(chances, grad, preferred_element_type=jnp.float32)
    query_turned = lax.dot_general(key, grad_score, COL_COL, preferred_element_type=jnp.float32)
    query_grad = (query_turned.T * SCALE).astype(jnp.bfloat16)
    return query_grad, key_term, value_term


def prompt_kernel(shared, table, q_ref, g_ref, k_ref, v_ref, dq_ref, dk_ref, dv_ref):
    @pl.when(pl.program_id(0) % shared == 0)
    def _():
        dk_ref[...] = jnp.zeros_like(dk_ref)
        dv_ref[...] = jnp.zeros_like(dv_ref)

    for begin in range(0, PROMPT, RESP):
        rows = pl.ds(begin, RESP)
        seen = pl.ds(0, begin + RESP)
        dq, dk, dv = attend(q_ref[rows, :], g_ref[rows, :], k_ref[seen, :], v_ref[seen, :])
        dq_ref[rows, :] = dq
        dk_ref[seen, :] += dk
        dv_ref[seen, :] += dv


def reply_kernel(
    shared, table, q_ref, g_ref, k_ref, v_ref, pk0, pv0, pk1, pv1, _, dq_ref, out_ref, dk_ref, dv_ref, kacc, vacc
):
    step = pl.program_id(0) % shared

    @pl.when(step == 0)
    def _():
        kacc[...] = jnp.zeros_like(kacc)
        vacc[...] = jnp.zeros_like(vacc)

    index = lax.broadcasted_iota(jnp.int32, (RESP, 1), 0)
    for slot in range(2):
        rows = pl.ds(slot * RESP, RESP)
        prompt_key, prompt_value = ((pk0, pv0), (pk1, pv1))[slot]
        grad = jnp.where(index < table[3 + slot], g_ref[rows, :], jnp.zeros((), jnp.bfloat16))
        key = jnp.concatenate([prompt_key[0], k_ref[rows, :]], axis=0)
        value = jnp.concatenate([prompt_value[0], v_ref[rows, :]], axis=0)
        dq, dk, dv = attend(q_ref[rows, :], grad, key, value)
        dq_ref[rows, :] = dq
        kacc[slot] += dk
        vacc[slot] += dv

    @pl.when(step == shared - 1)
    def _():
        for slot in range(2):
            rows = pl.ds(slot * RESP, RESP)
            dk_ref[rows, :] = kacc[slot, PROMPT:]
            dv_ref[rows, :] = vacc[slot, PROMPT:]
        for peer in range(out_ref.shape[0]):
            for column, acc in ((0, kacc), (HD, vacc)):
                first = jnp.where(table[1] == peer, acc[0, :PROMPT], 0.0)
                second = jnp.where(table[2] == peer, acc[1, :PROMPT], 0.0)
                out_ref[peer, :, column : column + HD] = (first + second).astype(jnp.bfloat16)


def per_device(queries, keys, values, out_grad, prompt_group, slot_group, resp_len):
    seq_count = lax.axis_size("seq")
    local_heads = queries.shape[1] // HD
    kv_local = keys.shape[1] // HD
    used = max(local_heads // (HQ // KVH), 1)
    shared = local_heads // used
    first_head = lax.axis_index("sub") * local_heads // (HQ // KVH) if used != kv_local else 0
    if used == kv_local:
        key_part, value_part = keys[:PROMPT], values[:PROMPT]
    else:
        key_part = lax.dynamic_slice(keys, (0, first_head * HD), (PROMPT, used * HD))
        value_part = lax.dynamic_slice(values, (0, first_head * HD), (PROMPT, used * HD))
    prompt_pair = jnp.concatenate([key_part, value_part], axis=1)
    every = lax.all_gather(prompt_pair[None], "seq", axis=0, tiled=True)
    peers = jnp.arange(seq_count, dtype=jnp.int32)
    owners = jnp.sum(
        peers[:, None] * (prompt_group[:, None] == peers[None, :]).astype(jnp.int32), axis=0
    )
    own_index = lax.axis_index("seq")
    my_slots = jnp.sum(slot_group * (peers[:, None] == own_index).astype(jnp.int32), axis=0)
    my_owner = jnp.sum(
        owners[None, :] * (my_slots[:, None] == peers[None, :]).astype(jnp.int32), axis=1
    )
    table = jnp.concatenate(
        [jnp.full((1,), first_head, jnp.int32), my_owner, resp_len[0]]
    ).astype(jnp.int32)

    def head_block(row):
        return pl.BlockSpec((PROMPT, HD), lambda h, t: (row, h))

    def kv_block(row):
        return pl.BlockSpec((PROMPT, HD), lambda h, t: (row, t[0] + h // shared))

    sum_block = pl.BlockSpec((PROMPT, HD), lambda h, t: (0, h // shared))

    def fetched_block(slot, offset):
        return pl.BlockSpec((1, PROMPT, HD), lambda h, t: (t[1 + slot], 0, offset + h // shared))

    params = pltpu.CompilerParams(
        dimension_semantics=("arbitrary",), vmem_limit_bytes=40 * 1024 * 1024
    )
    grad_shape = jax.ShapeDtypeStruct((PROMPT, used * HD), jnp.float32)
    query_shape = jax.ShapeDtypeStruct(queries.shape, jnp.bfloat16)
    work = local_heads * RESP * RESP * HD * 10
    query_half, prompt_dk, prompt_dv = pl.pallas_call(
        functools.partial(prompt_kernel, shared),
        grid_spec=pltpu.PrefetchScalarGridSpec(
            num_scalar_prefetch=1,
            grid=(local_heads,),
            in_specs=[head_block(0), head_block(0), kv_block(0), kv_block(0)],
            out_specs=[head_block(0), sum_block, sum_block],
        ),
        out_shape=[query_shape, grad_shape, grad_shape],
        compiler_params=params,
        cost_estimate=pl.CostEstimate(
            flops=work * 3 * 2, bytes_accessed=8 << 20, transcendentals=0
        ),
    )(table, queries, out_grad, keys, values)
    query_total, outgoing, reply_dk, reply_dv = pl.pallas_call(
        functools.partial(reply_kernel, shared),
        grid_spec=pltpu.PrefetchScalarGridSpec(
            num_scalar_prefetch=1,
            grid=(local_heads,),
            in_specs=[head_block(1), head_block(1), kv_block(1), kv_block(1)]
            + [fetched_block(slot, offset) for slot in range(2) for offset in (0, used)]
            + [pl.BlockSpec(memory_space=pl.ANY)],
            out_specs=[
                head_block(1),
                pl.BlockSpec((seq_count, PROMPT, 2 * HD), lambda h, t: (0, 0, h // shared)),
                sum_block,
                sum_block,
            ],
            scratch_shapes=[pltpu.VMEM((2, PROMPT + RESP, HD), jnp.float32)] * 2,
        ),
        out_shape=[
            query_shape,
            jax.ShapeDtypeStruct((seq_count, PROMPT, used * 2 * HD), jnp.bfloat16),
            grad_shape,
            grad_shape,
        ],
        input_output_aliases={9: 0},
        compiler_params=params,
        cost_estimate=pl.CostEstimate(
            flops=work * 6 * 2, bytes_accessed=8 << 20, transcendentals=0
        ),
    )(table, queries, out_grad, keys, values, every, every, every, every, query_half)
    arrived = lax.all_to_all(outgoing, "seq", split_axis=0, concat_axis=0, tiled=True)
    returned = jnp.sum(arrived.astype(jnp.float32), axis=0).reshape(PROMPT, used, 2, HD)
    key_top = prompt_dk + returned[:, :, 0].reshape(PROMPT, used * HD)
    value_top = prompt_dv + returned[:, :, 1].reshape(PROMPT, used * HD)

    def across(rows):
        mine = rows.astype(jnp.bfloat16)
        if used == kv_local:
            return lax.psum(mine, "sub").astype(jnp.bfloat16)
        other = lax.ppermute(mine, "sub", [(0, 1), (1, 0)])
        front = lax.axis_index("sub") == 0
        return jnp.concatenate(
            [jnp.where(front, mine, other), jnp.where(front, other, mine)], axis=1
        )

    top = across(jnp.concatenate([key_top, value_top], axis=0))
    low = across(jnp.concatenate([reply_dk, reply_dv], axis=0))
    key_total = jnp.concatenate([top[:PROMPT], low[:PROMPT]], axis=0)
    value_total = jnp.concatenate([top[PROMPT:], low[PROMPT:]], axis=0)
    return (query_total, key_total, value_total)


def solution(mesh):
    placed = (
        P(("parts", "seq"), ("head", "sub")),
        P(("parts", "seq"), "head"),
        P(("parts", "seq"), "head"),
        P(("parts", "seq"), ("head", "sub")),
        P("parts"),
        P("parts", None),
        P(("parts", "seq"), None),
    )
    return jax.shard_map(
        per_device,
        mesh=mesh,
        in_specs=placed,
        out_specs=(
            P(("parts", "seq"), ("head", "sub")),
            P(("parts", "seq"), "head"),
            P(("parts", "seq"), "head"),
        ),
        check_vma=False,
    )
```

```python
import functools
import math

import jax
import jax.numpy as jnp
from jax import lax
from jax.experimental import pallas as pl
from jax.experimental.pallas import tpu as pltpu
from jax.sharding import PartitionSpec as P

HQ = 64
KVH = 8
HD = 128
PROMPT = 512
RESP = 256
SCALE = 1.0 / math.sqrt(HD)
EXP2_SCALE = SCALE * math.log2(math.e)
ROW_ROW = (((1,), (1,)), ((), ()))
MESH = pl.DeviceIdType.MESH


def attend(query, grad, key, value, key_turned):
    extent, amount = key.shape[0], query.shape[0]
    scores = lax.dot_general(key, query, ROW_ROW, preferred_element_type=jnp.float32)
    grad_chance = lax.dot_general(value, grad, ROW_ROW, preferred_element_type=jnp.float32)
    key_index = lax.broadcasted_iota(jnp.int32, (amount, amount), 0)
    query_index = lax.broadcasted_iota(jnp.int32, (amount, amount), 1)
    last = jnp.where(key_index <= query_index, scores[extent - amount :], -jnp.inf)
    if extent > amount:
        scores = jnp.concatenate([scores[: extent - amount], last], axis=0)
    else:
        scores = last
    highest = jnp.max(scores, axis=0, keepdims=True)
    weights = jnp.exp2((scores - highest) * EXP2_SCALE)
    inverse = 1.0 / jnp.sum(weights, axis=0, keepdims=True)
    row_dot = jnp.sum(weights * grad_chance, axis=0, keepdims=True) * inverse
    chances = (weights * inverse).astype(jnp.bfloat16)
    grad_score = chances * (grad_chance - row_dot).astype(jnp.bfloat16)
    key_term = jnp.dot(grad_score, query, preferred_element_type=jnp.float32)
    value_term = jnp.dot(chances, grad, preferred_element_type=jnp.float32)
    query_turned = jnp.dot(key_turned, grad_score, preferred_element_type=jnp.float32)
    query_grad = (query_turned.T * SCALE).astype(jnp.bfloat16)
    return query_grad, key_term, value_term


def fused(plan, table, q_hbm, g_hbm, k_hbm, v_hbm, dq_hbm, dk_hbm, dv_hbm, *scratch):
    count, used, shared, kv_local = plan
    (q, g, dq, own, key_turned, joined, joined_turned, prompt_acc, reply_acc, final, load_sem, store_sem) = scratch[:12]
    (gather_send, gather_recv, back_send, back_recv, sub_send, sub_recv) = scratch[12:18]
    every = scratch[18 : 18 + used]
    outgoing = scratch[18 + used : 18 + 2 * used]
    arrived = scratch[18 + 2 * used : 18 + 3 * used]
    partner_terms = scratch[18 + 3 * used :]
    me = lax.axis_index("seq")
    sub = lax.axis_index("sub")
    split = used != kv_local
    first_head = sub * used if split else 0
    width = shared * HD
    peers = [lax.rem(me + step, count) for step in range(count)]
    kv_hbm, dkv_hbm = (k_hbm, v_hbm), (dk_hbm, dv_hbm)

    def columns(head):
        return pl.ds(pl.multiple_of((first_head + head) * HD, HD), HD)

    loads = {}
    for head in range(used):
        for which in range(2):
            copy = pltpu.make_async_copy(
                kv_hbm[which].at[:, columns(head)], own.at[head, which], load_sem.at[head, 4 + which]
            )
            copy.start()
            loads[head, 4 + which] = copy
    for head in range(used):
        for half in range(2):
            rows = pl.ds(half * PROMPT, PROMPT)
            place = pl.ds(head * width, width)
            for which, source, target in ((0, q_hbm, q), (1, g_hbm, g)):
                copy = pltpu.make_async_copy(
                    source.at[rows, place], target.at[rows, place], load_sem.at[head, 2 * half + which]
                )
                copy.start()
                loads[head, 2 * half + which] = copy

    barrier = pltpu.get_barrier_semaphore()
    for peer in peers[1:]:
        pl.semaphore_signal(barrier, inc=1, device_id={"seq": peer}, device_id_type=MESH)
    pl.semaphore_signal(barrier, inc=1, device_id={"sub": 1 - sub}, device_id_type=MESH)
    pl.semaphore_wait(barrier, count)

    gathers = []
    for head in range(used):
        group = []
        for which in range(2):
            for step in range(1, count):
                copy = pltpu.make_async_remote_copy(
                    src_ref=kv_hbm[which].at[pl.ds(0, PROMPT), columns(head)],
                    dst_ref=every[head].at[me, which],
                    send_sem=gather_send.at[head, which, step],
                    recv_sem=gather_recv.at[head, which, step],
                    device_id={"seq": peers[step]},
                    device_id_type=MESH,
                )
                copy.start()
                group.append(copy)
        gathers.append(group)

    prompt_acc[...] = jnp.zeros_like(prompt_acc)

    def head_place(head, member):
        return pl.ds(pl.multiple_of(head * width + member * HD, HD), HD)

    def prompt_work(head, begin, finish):
        if begin == 0:
            for index in (4, 5, 0, 1):
                loads[head, index].wait()
            key_turned[...] = own[head, 0, :PROMPT].T

        @pl.loop(begin, finish)
        def _(member):
            place = head_place(head, member)
            for start in range(0, PROMPT, RESP):
                rows, seen = pl.ds(start, RESP), pl.ds(0, start + RESP)
                dq[rows, place], key_term, value_term = attend(
                    q[rows, place], g[rows, place], own[head, 0, seen], own[head, 1, seen], key_turned[:, seen]
                )
                prompt_acc[head, 0, seen] += key_term
                prompt_acc[head, 1, seen] += value_term

        return store_query(head, 0) if finish == shared else None

    def store_query(head, half):
        rows, place = pl.ds(half * PROMPT, PROMPT), pl.ds(head * width, width)
        copy = pltpu.make_async_copy(
            dq.at[rows, place], dq_hbm.at[rows, place], store_sem.at[head, half]
        )
        copy.start()
        return copy

    def reply_work(head):
        for which in range(2):
            every[head][me, which] = own[head, which, :PROMPT]
        for copy in gathers[head]:
            copy.wait()
        for slot in range(2):
            for which in range(2):
                joined[slot, which, :PROMPT] = every[head][table[slot], which]
                joined[slot, which, PROMPT:] = own[head, which, PROMPT + slot * RESP : PROMPT + (slot + 1) * RESP]
            joined_turned[slot] = joined[slot, 0].T
        loads[head, 2].wait()
        loads[head, 3].wait()
        reply_acc[...] = jnp.zeros_like(reply_acc)
        live_index = lax.broadcasted_iota(jnp.int32, (RESP, 1), 0)

        @pl.loop(0, shared)
        def _(member):
            place = head_place(head, member)
            for slot in range(2):
                rows = pl.ds(PROMPT + slot * RESP, RESP)
                live = jnp.where(live_index < table[2 + slot], g[rows, place], jnp.zeros((), jnp.bfloat16))
                dq[rows, place], key_term, value_term = attend(
                    q[rows, place], live, joined[slot, 0], joined[slot, 1], joined_turned[slot]
                )
                reply_acc[slot, 0] += key_term
                reply_acc[slot, 1] += value_term

        copies = []
        for step in range(count):
            for which in range(2):
                total = jnp.where(table[0] == peers[step], reply_acc[0, which, :PROMPT], 0.0) + jnp.where(
                    table[1] == peers[step], reply_acc[1, which, :PROMPT], 0.0
                )
                if step == 0:
                    prompt_acc[head, which] += total
                else:
                    factor = (SCALE, 1.0)[which]
                    outgoing[head][step, which] = (total * factor).astype(jnp.bfloat16)
            if step:
                copy = pltpu.make_async_remote_copy(
                    src_ref=outgoing[head].at[step],
                    dst_ref=arrived[head].at[step],
                    send_sem=back_send.at[head, step],
                    recv_sem=back_recv.at[head, step],
                    device_id={"seq": peers[step]},
                    device_id_type=MESH,
                )
                copy.start()
                copies.append(copy)
        for which in range(2):
            for slot in range(2):
                total = reply_acc[slot, which, PROMPT:] * (SCALE, 1.0)[which]
                final[head, which, PROMPT + slot * RESP : PROMPT + (slot + 1) * RESP] = total.astype(jnp.bfloat16)
        return copies, store_query(head, 1), share(head, 1)

    def share(head, half):
        rows = pl.ds(half * PROMPT, PROMPT)
        copies = []
        for which in range(2):
            source = final.at[head, which, rows]
            target = dkv_hbm[which].at[rows, columns(head)] if split else partner_terms[0].at[head, which, rows]
            remote = pltpu.make_async_remote_copy(
                src_ref=source,
                dst_ref=target,
                send_sem=sub_send.at[head, which, half],
                recv_sem=sub_recv.at[head, which, half],
                device_id={"sub": 1 - sub},
                device_id_type=MESH,
            )
            remote.start()
            copies.append(remote)
            if split:
                local = pltpu.make_async_copy(source, target, store_sem.at[head, 2 + 2 * which + half])
                local.start()
                copies.append(local)
        return copies

    pending = []
    early = shared // 2 if used > 1 else 0
    pending.append(prompt_work(0, 0, shared))
    if early:
        prompt_work(1, 0, early)
    backs = []
    for head in range(used):
        copies, stored, shares = reply_work(head)
        backs.append(copies)
        pending.append(stored)
        pending.extend(shares)
    for head in range(1, used):
        pending.append(prompt_work(head, early if head == 1 else 0, shared))
    for head in range(used):
        for copy in backs[head]:
            copy.wait()
        for which in range(2):
            total = prompt_acc[head, which] * (SCALE, 1.0)[which]
            for step in range(1, count):
                total += arrived[head][step, which].astype(jnp.float32)
            final[head, which, :PROMPT] = total.astype(jnp.bfloat16)
        pending.extend(share(head, 0))
    for copy in pending:
        copy.wait()
    if not split:
        for head in range(used):
            for which in range(2):
                mine = final[head, which].astype(jnp.float32)
                both = mine + partner_terms[0][head, which].astype(jnp.float32)
                final[head, which] = both.astype(jnp.bfloat16)
                copy = pltpu.make_async_copy(
                    final.at[head, which], dkv_hbm[which].at[:, columns(head)], store_sem.at[head, 2 + which]
                )
                copy.start()
                copy.wait()


def per_device(queries, keys, values, out_grad, prompt_group, slot_group, resp_len):
    seq_count = lax.axis_size("seq")
    local_heads = queries.shape[1] // HD
    kv_local = keys.shape[1] // HD
    used = max(local_heads // (HQ // KVH), 1)
    shared = local_heads // used
    total_rows = queries.shape[0]
    peers = jnp.arange(seq_count, dtype=jnp.int32)
    owners = jnp.sum(
        peers[:, None] * (prompt_group[:, None] == peers[None, :]).astype(jnp.int32), axis=0
    )
    own_index = lax.axis_index("seq")
    my_slots = jnp.sum(slot_group * (peers[:, None] == own_index).astype(jnp.int32), axis=0)
    my_owner = jnp.sum(
        owners[None, :] * (my_slots[:, None] == peers[None, :]).astype(jnp.int32), axis=1
    )
    table = jnp.concatenate([my_owner, resp_len[0]]).astype(jnp.int32)
    anywhere = pl.BlockSpec(memory_space=pl.ANY)
    bf16, f32 = jnp.bfloat16, jnp.float32
    dma = pltpu.SemaphoreType.DMA
    exchanged = [pltpu.VMEM((seq_count, 2, PROMPT, HD), bf16)] * (3 * used)
    partner = [] if used != kv_local else [pltpu.VMEM((used, 2, total_rows, HD), bf16)]
    return pl.pallas_call(
        functools.partial(fused, (seq_count, used, shared, kv_local)),
        in_specs=[pl.BlockSpec(memory_space=pltpu.SMEM)] + [anywhere] * 4,
        out_specs=[anywhere] * 3,
        out_shape=[jax.ShapeDtypeStruct(array.shape, bf16) for array in (queries, keys, values)],
        scratch_shapes=[
            pltpu.VMEM(queries.shape, bf16),
            pltpu.VMEM(queries.shape, bf16),
            pltpu.VMEM(queries.shape, bf16),
            pltpu.VMEM((used, 2, total_rows, HD), bf16),
            pltpu.VMEM((HD, PROMPT), bf16),
            pltpu.VMEM((2, 2, PROMPT + RESP, HD), bf16),
            pltpu.VMEM((2, HD, PROMPT + RESP), bf16),
            pltpu.VMEM((used, 2, PROMPT, HD), f32),
            pltpu.VMEM((2, 2, PROMPT + RESP, HD), f32),
            pltpu.VMEM((used, 2, total_rows, HD), bf16),
            dma((used, 6)),
            dma((used, 6)),
            dma((used, 2, seq_count)),
            dma((used, 2, seq_count)),
            dma((used, seq_count)),
            dma((used, seq_count)),
            dma((used, 2, 2)),
            dma((used, 2, 2)),
        ]
        + exchanged
        + partner,
        compiler_params=pltpu.CompilerParams(
            collective_id=0, has_side_effects=True, vmem_limit_bytes=56 * 1024 * 1024
        ),
    )(table, queries, out_grad, keys, values)


def solution(mesh):
    placed = (
        P(("parts", "seq"), ("head", "sub")),
        P(("parts", "seq"), "head"),
        P(("parts", "seq"), "head"),
        P(("parts", "seq"), ("head", "sub")),
        P("parts"),
        P("parts", None),
        P(("parts", "seq"), None),
    )
    return jax.shard_map(
        per_device,
        mesh=mesh,
        in_specs=placed,
        out_specs=(
            P(("parts", "seq"), ("head", "sub")),
            P(("parts", "seq"), "head"),
            P(("parts", "seq"), "head"),
        ),
        check_vma=False,
    )
```

```python
import functools
import math

import jax
import jax.numpy as jnp
from jax import lax
from jax.experimental import pallas as pl
from jax.experimental.pallas import tpu as pltpu
from jax.sharding import PartitionSpec as P

HQ = 64
KVH = 8
HD = 128
PROMPT = 512
RESP = 256
SCALE = 1.0 / math.sqrt(HD)
EARLY = 2
EXP2_SCALE = SCALE * math.log2(math.e)
ROW_ROW = (((1,), (1,)), ((), ()))
MESH = pl.DeviceIdType.MESH


def attend(query, grad, key, value, key_turned):
    extent, amount = key.shape[0], query.shape[0]
    scores = lax.dot_general(key, query, ROW_ROW, preferred_element_type=jnp.float32)
    grad_chance = lax.dot_general(value, grad, ROW_ROW, preferred_element_type=jnp.float32)
    key_index = lax.broadcasted_iota(jnp.int32, (amount, amount), 0)
    query_index = lax.broadcasted_iota(jnp.int32, (amount, amount), 1)
    last = jnp.where(key_index <= query_index, scores[extent - amount :], -jnp.inf)
    if extent > amount:
        scores = jnp.concatenate([scores[: extent - amount], last], axis=0)
    else:
        scores = last
    highest = jnp.max(scores, axis=0, keepdims=True)
    weights = jnp.exp2((scores - highest) * EXP2_SCALE)
    inverse = 1.0 / jnp.sum(weights, axis=0, keepdims=True)
    row_dot = jnp.sum(weights * grad_chance, axis=0, keepdims=True) * inverse
    chances = (weights * inverse).astype(jnp.bfloat16)
    grad_score = chances * (grad_chance - row_dot).astype(jnp.bfloat16)
    key_term = jnp.dot(grad_score, query, preferred_element_type=jnp.float32)
    value_term = jnp.dot(chances, grad, preferred_element_type=jnp.float32)
    query_turned = jnp.dot(key_turned, grad_score, preferred_element_type=jnp.float32)
    query_grad = (query_turned.T * SCALE).astype(jnp.bfloat16)
    return query_grad, key_term, value_term


def fused(plan, table, q_hbm, g_hbm, k_hbm, v_hbm, dq_hbm, dk_hbm, dv_hbm, *scratch):
    count, used, shared, kv_local = plan
    (q, g, dq, own, key_turned, joined, joined_turned, prompt_acc, reply_acc, final, load_sem, store_sem) = scratch[:12]
    (gather_send, gather_recv, back_send, back_recv, sub_send, sub_recv) = scratch[12:18]
    every = scratch[18 : 18 + used]
    terms, sent, arrived = scratch[18 + used : 21 + used]
    partner_terms = scratch[21 + used :]
    me = lax.axis_index("seq")
    sub = lax.axis_index("sub")
    split = used != kv_local
    first_head = sub * used if split else 0
    width = shared * HD
    kv_hbm, dkv_hbm = (k_hbm, v_hbm), (dk_hbm, dv_hbm)

    def columns(head):
        return pl.ds(pl.multiple_of((first_head + head) * HD, HD), HD)

    loads = {}
    for head in range(used):
        for which in range(2):
            copy = pltpu.make_async_copy(
                kv_hbm[which].at[:, columns(head)], own.at[head, which], load_sem.at[head, 4 + which]
            )
            copy.start()
            loads[head, 4 + which] = copy
    for head in range(used):
        for half in range(2):
            rows = pl.ds(half * PROMPT, PROMPT)
            place = pl.ds(head * width, width)
            for which, source, target in ((0, q_hbm, q), (1, g_hbm, g)):
                copy = pltpu.make_async_copy(
                    source.at[rows, place], target.at[rows, place], load_sem.at[head, 2 * half + which]
                )
                copy.start()
                loads[head, 2 * half + which] = copy

    barrier = pltpu.get_barrier_semaphore()
    ways = [(0, me, 1), (1, count - 1 - me, -1)]
    for _, rank, sign in ways:

        @pl.when(rank < count - 1)
        def _():
            pl.semaphore_signal(barrier, inc=1, device_id={"seq": me + sign}, device_id_type=MESH)

    pl.semaphore_signal(barrier, inc=1, device_id={"sub": 1 - sub}, device_id_type=MESH)
    near = jnp.where(me > 0, 1, 0) + jnp.where(me < count - 1, 1, 0)
    pl.semaphore_wait(barrier, near + 1)

    def gather_copy(head, way, sign, tick, first):
        block = me - sign * tick
        return pltpu.make_async_remote_copy(
            src_ref=own.at[head, :, pl.ds(0, PROMPT)] if first else every[head].at[block],
            dst_ref=every[head].at[block],
            send_sem=gather_send.at[head, way, tick],
            recv_sem=gather_recv.at[head, way, tick],
            device_id={"seq": me + sign},
            device_id_type=MESH,
        )

    def gather_arrival(head, way, sign, tick):
        block = every[head].at[me - sign * tick]
        return pltpu.make_async_remote_copy(
            src_ref=block,
            dst_ref=block,
            send_sem=gather_send.at[head, way, tick],
            recv_sem=gather_recv.at[head, way, tick - 1],
            device_id={"seq": me - sign},
            device_id_type=MESH,
        )

    def gather_first(head):
        for way, rank, sign in ways:

            @pl.when(rank < count - 1)
            def _():
                gather_copy(head, way, sign, 0, True).start()

    def gather_tick(head, tick):
        for way, rank, sign in ways:

            @pl.when(tick <= rank)
            def _():
                gather_arrival(head, way, sign, tick).wait_recv()

            @pl.when((tick <= rank) & (rank < count - 1))
            def _():
                gather_copy(head, way, sign, tick, False).start()

    def back_copy(head, way, sign, tick):
        return pltpu.make_async_remote_copy(
            src_ref=sent.at[head, way, tick],
            dst_ref=arrived.at[head, way, tick],
            send_sem=back_send.at[head, way, tick],
            recv_sem=back_recv.at[head, way, tick],
            device_id={"seq": me + sign},
            device_id_type=MESH,
        )

    def term_for(head, which, target):
        return jnp.where(table[0] == target, terms[head, 0, which].astype(jnp.float32), 0.0) + jnp.where(
            table[1] == target, terms[head, 1, which].astype(jnp.float32), 0.0
        )

    def back_first(head):
        for way, rank, sign in ways:

            @pl.when(rank == 0)
            def _():
                for which in range(2):
                    total = term_for(head, which, me + sign * (count - 1))
                    sent[head, way, 0, which] = total.astype(jnp.bfloat16)
                back_copy(head, way, sign, 0).start()

    def back_tick(head, tick):
        for way, rank, sign in ways:
            target = me + sign * (count - 1 - tick)

            @pl.when((tick >= rank) & (rank > 0))
            def _():
                pltpu.make_async_remote_copy(
                    src_ref=arrived.at[head, way, tick - 1],
                    dst_ref=arrived.at[head, way, tick - 1],
                    send_sem=back_send.at[head, way, tick],
                    recv_sem=back_recv.at[head, way, tick - 1],
                    device_id={"seq": me - sign},
                    device_id_type=MESH,
                ).wait_recv()

            @pl.when((tick >= rank) & (rank > 0) & (tick < count - 1))
            def _():
                for which in range(2):
                    total = term_for(head, which, target) + arrived[head, way, tick - 1, which].astype(jnp.float32)
                    sent[head, way, tick, which] = total.astype(jnp.bfloat16)
                back_copy(head, way, sign, tick).start()

            @pl.when((rank == 0) & (tick < count - 1))
            def _():
                for which in range(2):
                    sent[head, way, tick, which] = term_for(head, which, target).astype(jnp.bfloat16)
                back_copy(head, way, sign, tick).start()

            @pl.when((rank > 0) & (tick == count - 1))
            def _():
                for which in range(2):
                    prompt_acc[head, which] += arrived[head, way, count - 2, which].astype(jnp.float32)

    def finish_sends():
        for head in range(used):
            for way, rank, sign in ways:

                @pl.loop(0, count - 1)
                def _(tick):
                    @pl.when((tick <= rank) & (rank < count - 1))
                    def _():
                        gather_copy(head, way, sign, tick, False).wait_send()

                    @pl.when(tick >= rank)
                    def _():
                        back_copy(head, way, sign, tick).wait_send()

    def members(begin, finish, work, ticker=None, interval=1):
        @pl.loop(begin, finish)
        def _(member):
            work(member)
            if ticker is not None:
                passed = member - begin + 1
                tick = passed // interval

                @pl.when((passed % interval == 0) & (tick < count))
                def _():
                    ticker(tick)

        return 1 + ((finish - begin) // interval if ticker is not None else 0)

    def flush(ticker, tick):
        if tick < count:

            @pl.loop(tick, count)
            def _(later):
                ticker(later)

    for head in range(used):
        loads[head, 4].wait()
        loads[head, 5].wait()
        if head == 0:
            gather_first(0)
    prompt_acc[...] = jnp.zeros_like(prompt_acc)

    def head_place(head, member):
        return pl.ds(pl.multiple_of(head * width + member * HD, HD), HD)

    def prompt_work(head, begin, finish, ticker=None, interval=1):
        if begin == 0:
            for index in (0, 1):
                loads[head, index].wait()
            key_turned[...] = own[head, 0, :PROMPT].T

        def work(member):
            place = head_place(head, member)
            for start in range(0, PROMPT, RESP):
                rows, seen = pl.ds(start, RESP), pl.ds(0, start + RESP)
                dq[rows, place], key_term, value_term = attend(
                    q[rows, place], g[rows, place], own[head, 0, seen], own[head, 1, seen], key_turned[:, seen]
                )
                prompt_acc[head, 0, seen] += key_term
                prompt_acc[head, 1, seen] += value_term

        tick = members(begin, finish, work, ticker, interval)
        if finish == shared:
            pending.append(store_query(head, 0))
        return tick

    def store_query(head, half):
        rows, place = pl.ds(half * PROMPT, PROMPT), pl.ds(head * width, width)
        copy = pltpu.make_async_copy(
            dq.at[rows, place], dq_hbm.at[rows, place], store_sem.at[head, half]
        )
        copy.start()
        return copy

    def reply_work(head, ticker=None, interval=1):
        for which in range(2):
            every[head][me, which] = own[head, which, :PROMPT]
        for slot in range(2):
            for which in range(2):
                joined[slot, which, :PROMPT] = every[head][table[slot], which]
                joined[slot, which, PROMPT:] = own[head, which, PROMPT + slot * RESP : PROMPT + (slot + 1) * RESP]
            joined_turned[slot] = joined[slot, 0].T
        loads[head, 2].wait()
        loads[head, 3].wait()
        reply_acc[...] = jnp.zeros_like(reply_acc)
        live_index = lax.broadcasted_iota(jnp.int32, (RESP, 1), 0)

        def work(member):
            place = head_place(head, member)
            for slot in range(2):
                rows = pl.ds(PROMPT + slot * RESP, RESP)
                live = jnp.where(live_index < table[2 + slot], g[rows, place], jnp.zeros((), jnp.bfloat16))
                dq[rows, place], key_term, value_term = attend(
                    q[rows, place], live, joined[slot, 0], joined[slot, 1], joined_turned[slot]
                )
                reply_acc[slot, 0] += key_term
                reply_acc[slot, 1] += value_term

        tick = members(0, shared, work, ticker, interval)
        for which in range(2):
            for slot in range(2):
                total = reply_acc[slot, which, :PROMPT]
                terms[head, slot, which] = total.astype(jnp.bfloat16)
                prompt_acc[head, which] += jnp.where(table[slot] == me, total, 0.0)
        back_first(head)
        for which in range(2):
            for slot in range(2):
                total = reply_acc[slot, which, PROMPT:] * (SCALE, 1.0)[which]
                final[head, which, PROMPT + slot * RESP : PROMPT + (slot + 1) * RESP] = total.astype(jnp.bfloat16)
        pending.append(store_query(head, 1))
        pending.extend(share(head, 1))
        return tick

    def share(head, half):
        rows = pl.ds(half * PROMPT, PROMPT)
        copies = []
        for which in range(2):
            source = final.at[head, which, rows]
            target = dkv_hbm[which].at[rows, columns(head)] if split else partner_terms[0].at[head, which, rows]
            remote = pltpu.make_async_remote_copy(
                src_ref=source,
                dst_ref=target,
                send_sem=sub_send.at[head, which, half],
                recv_sem=sub_recv.at[head, which, half],
                device_id={"sub": 1 - sub},
                device_id_type=MESH,
            )
            remote.start()
            copies.append(remote)
            if split:
                local = pltpu.make_async_copy(source, target, store_sem.at[head, 2 + 2 * which + half])
                local.start()
                copies.append(local)
        return copies

    pending = []

    def gather_of(head):
        return lambda tick: gather_tick(head, tick)

    def back_of(head):
        return lambda tick: back_tick(head, tick)

    early = EARLY if used > 1 else 0
    tick = prompt_work(0, 0, shared, gather_of(0), 4)
    if used > 1:
        gather_first(1)
        if early:
            prompt_work(1, 0, early)
    flush(gather_of(0), tick)
    for head in range(used):
        if head == 0 and used > 1:
            flush(gather_of(1), reply_work(0, gather_of(1), 2))
        elif head == 0:
            reply_work(0)
        else:
            if head > 1:
                gather_first(head)
                flush(gather_of(head), 1)
            flush(back_of(head - 1), reply_work(head, back_of(head - 1), 2))
    tick = 1
    for head in range(1, used):
        ticker = back_of(used - 1) if head == 1 else None
        passed = prompt_work(head, early if head == 1 else 0, shared, ticker, 3)
        tick = passed if head == 1 else tick
    flush(back_of(used - 1), tick)
    finish_sends()
    for head in range(used):
        for which in range(2):
            total = prompt_acc[head, which] * (SCALE, 1.0)[which]
            final[head, which, :PROMPT] = total.astype(jnp.bfloat16)
        pending.extend(share(head, 0))
    for copy in pending:
        copy.wait()
    if not split:
        for head in range(used):
            for which in range(2):
                mine = final[head, which].astype(jnp.float32)
                both = mine + partner_terms[0][head, which].astype(jnp.float32)
                final[head, which] = both.astype(jnp.bfloat16)
                copy = pltpu.make_async_copy(
                    final.at[head, which], dkv_hbm[which].at[:, columns(head)], store_sem.at[head, 2 + which]
                )
                copy.start()
                copy.wait()


def per_device(queries, keys, values, out_grad, prompt_group, slot_group, resp_len):
    seq_count = lax.axis_size("seq")
    local_heads = queries.shape[1] // HD
    kv_local = keys.shape[1] // HD
    used = max(local_heads // (HQ // KVH), 1)
    shared = local_heads // used
    total_rows = queries.shape[0]
    peers = jnp.arange(seq_count, dtype=jnp.int32)
    owners = jnp.sum(
        peers[:, None] * (prompt_group[:, None] == peers[None, :]).astype(jnp.int32), axis=0
    )
    own_index = lax.axis_index("seq")
    my_slots = jnp.sum(slot_group * (peers[:, None] == own_index).astype(jnp.int32), axis=0)
    my_owner = jnp.sum(
        owners[None, :] * (my_slots[:, None] == peers[None, :]).astype(jnp.int32), axis=1
    )
    table = jnp.concatenate([my_owner, resp_len[0]]).astype(jnp.int32)
    anywhere = pl.BlockSpec(memory_space=pl.ANY)
    bf16, f32 = jnp.bfloat16, jnp.float32
    dma = pltpu.SemaphoreType.DMA
    exchanged = [pltpu.VMEM((seq_count, 2, PROMPT, HD), bf16)] * used
    exchanged += [pltpu.VMEM((used, 2, 2, PROMPT, HD), bf16)]
    exchanged += [pltpu.VMEM((used, 2, seq_count, 2, PROMPT, HD), bf16)] * 2
    partner = [] if used != kv_local else [pltpu.VMEM((used, 2, total_rows, HD), bf16)]
    return pl.pallas_call(
        functools.partial(fused, (seq_count, used, shared, kv_local)),
        in_specs=[pl.BlockSpec(memory_space=pltpu.SMEM)] + [anywhere] * 4,
        out_specs=[anywhere] * 3,
        out_shape=[jax.ShapeDtypeStruct(array.shape, bf16) for array in (queries, keys, values)],
        scratch_shapes=[
            pltpu.VMEM(queries.shape, bf16),
            pltpu.VMEM(queries.shape, bf16),
            pltpu.VMEM(queries.shape, bf16),
            pltpu.VMEM((used, 2, total_rows, HD), bf16),
            pltpu.VMEM((HD, PROMPT), bf16),
            pltpu.VMEM((2, 2, PROMPT + RESP, HD), bf16),
            pltpu.VMEM((2, HD, PROMPT + RESP), bf16),
            pltpu.VMEM((used, 2, PROMPT, HD), f32),
            pltpu.VMEM((2, 2, PROMPT + RESP, HD), f32),
            pltpu.VMEM((used, 2, total_rows, HD), bf16),
            dma((used, 6)),
            dma((used, 6)),
            dma((used, 2, seq_count)),
            dma((used, 2, seq_count)),
            dma((used, 2, seq_count)),
            dma((used, 2, seq_count)),
            dma((used, 2, 2)),
            dma((used, 2, 2)),
        ]
        + exchanged
        + partner,
        compiler_params=pltpu.CompilerParams(
            collective_id=0, has_side_effects=True, vmem_limit_bytes=56 * 1024 * 1024
        ),
    )(table, queries, out_grad, keys, values)


def solution(mesh):
    placed = (
        P(("parts", "seq"), ("head", "sub")),
        P(("parts", "seq"), "head"),
        P(("parts", "seq"), "head"),
        P(("parts", "seq"), ("head", "sub")),
        P("parts"),
        P("parts", None),
        P(("parts", "seq"), None),
    )
    return jax.shard_map(
        per_device,
        mesh=mesh,
        in_specs=placed,
        out_specs=(
            P(("parts", "seq"), ("head", "sub")),
            P(("parts", "seq"), "head"),
            P(("parts", "seq"), "head"),
        ),
        check_vma=False,
    )
```
